32 devices in a mesh: grp: 2 (over x), exp: 4 (over z), tp: 4 (over y, core).
Axes of the slice: x: 2, y: 2, z: 4, core: 2. Of those that a mesh axis runs over, the one named last changes fastest.
Arguments:
- tokens: bfloat16 [256, 4096], P(('grp', 'exp'), 'tp'), may hold values from -6 to 6
- routes: int32 [256, 8], P(('grp', 'exp')), may hold values from 0 to 7, as said below
- gates: bfloat16 [256, 8], P(('grp', 'exp')), may hold values from 0.049804688 to 0.59765625
- w_gate: bfloat16 [8, 4096, 1536], P(('grp', 'exp'), None, 'tp'), may hold values from -0.09375 to 0.09375
- w_up: bfloat16 [8, 4096, 1536], P(('grp', 'exp'), None, 'tp'), may hold values from -0.09375 to 0.09375
- hidden_grad: bfloat16 [8, 256, 1536], P(('grp', 'exp'), None, 'tp'), may hold values from -6 to 6
Outputs:
- token_grad: bfloat16 [256, 4096], P(('grp', 'exp'), 'tp')
The draws below stay inside these ranges and needn't reach their ends.
Inputs may be any that keep to these rules, and one draw needn't show every extreme that they name: `routes`: each row names 8 different experts, half of them in each of exactly two node groups (group g holds experts g * 4 to g * 4 + 3); all rows of one index of grp and exp share one of their two groups; among those rows no expert is named more than 32 times, and some expert is named exactly 32 times there.
All inputs are finite; a program needn't handle non-finite values.
Results may differ from the reference program's by a relative error of at most 0.012.
Values may be sent and summed in bfloat16 or wider, within the bound.
A program may use at most 64 MiB of HBM per device.

```python
import math
import jax
import jax.numpy as jnp
from jax import lax

D = 4096
H = 1536
TOP = 8
TOK_DEV = 32
EXPERTS = 8
HT = 384
C_SEND = 32
SLOTS = 256
TOKENS = 256
N_GRP = 2
N_EXP = 4
N_TP = 4


def draw_routes(key, part):
    key = jax.random.fold_in(key, 11)
    first_key, second_key, order_key = jax.random.split(key, 3)
    blocks = N_GRP * N_EXP
    per_group = TOP // 2
    shared_group = jax.random.randint(first_key, (blocks,), 0, N_GRP)
    other_group = (shared_group[:, None] + 1 + jax.random.randint(second_key, (blocks, TOK_DEV), 0, N_GRP - 1)) % N_GRP
    order_keys = jax.random.split(order_key, blocks * N_GRP * 2)
    orders = jax.vmap(lambda one_key: jax.random.permutation(one_key, N_EXP))(order_keys)
    orders = orders.reshape(blocks, N_GRP, 2, N_EXP).astype(jnp.int32)
    block_index = jnp.arange(blocks, dtype=jnp.int32)
    shared_order = orders[block_index, shared_group, 0]
    first_pos = (jnp.arange(TOK_DEV, dtype=jnp.int32)[:, None] * per_group + jnp.arange(per_group, dtype=jnp.int32)[None, :]) % N_EXP
    first_members = shared_order[:, first_pos]
    first_ids = shared_group[:, None, None] * N_EXP + first_members
    other_onehot = (other_group[:, :, None] == jnp.arange(N_GRP, dtype=jnp.int32)[None, None, :]).astype(jnp.int32)
    other_rank = jnp.sum((jnp.cumsum(other_onehot, axis=1) - other_onehot) * other_onehot, axis=2).astype(jnp.int32)
    other_order = orders[block_index[:, None], other_group, 1]
    second_pos = (other_rank[:, :, None] * per_group + jnp.arange(per_group, dtype=jnp.int32)[None, None, :]) % N_EXP
    second_members = jnp.take_along_axis(other_order, second_pos, axis=2)
    second_ids = other_group[:, :, None] * N_EXP + second_members
    chosen = jnp.concatenate([first_ids, second_ids], axis=2)
    return chosen.reshape(TOKENS, TOP).astype(jnp.int32)


def shard_levels(own_key, shape, shards, low, high):
    factor_of = 1.0
    for axis_at, blocks in shards:
        heights = jax.random.uniform(jax.random.fold_in(jax.random.fold_in(own_key, 6), axis_at), (blocks,), jnp.float32, low / len(shards), high / len(shards))
        factor_of = factor_of * jnp.repeat(jnp.exp(heights), shape[axis_at] // blocks).reshape((-1,) + (1,) * (len(shape) - 1 - axis_at))
    return factor_of


def bell_draw(key, dims, spread, bound, pieces=(), kind=jnp.bfloat16):
    result = jax.random.normal(key, dims, jnp.float32) * spread
    if len(pieces) > 0:
        result = shard_levels(key, dims, pieces, -0.22, 0.18) * result
    return jnp.clip(result, min=-bound, max=bound).astype(kind)


def setup_inputs(seed: int = 0) -> dict:
    seeds = jax.random.split(jax.random.key(seed), 7)
    tokens = bell_draw(seeds[0], (TOKENS, D), 1.0, 6.0, ((0, 8), (1, 4)))
    routes = draw_routes(jax.random.fold_in(seeds[6], 71), 0)
    gates = jnp.clip(jnp.exp(math.log(0.59765625) - 2.4849066 * jax.random.uniform(seeds[2], (TOKENS, TOP), jnp.float32) ** shard_levels(seeds[2], (TOKENS, TOP), ((0, 8),), -0.2, 0.2)), 0.049804688, 0.59765625).astype(jnp.bfloat16)
    w_gate = bell_draw(seeds[3], (EXPERTS, D, H), D ** -0.5, 0.09375, ((0, 8), (2, 4)))
    w_up = bell_draw(seeds[4], (EXPERTS, D, H), D ** -0.5, 0.09375, ((0, 8), (2, 4)))
    hidden_grad = bell_draw(seeds[5], (EXPERTS, SLOTS, H), 1.0, 6.0, ((0, 8), (2, 4)))
    return dict(tokens=tokens, routes=routes, gates=gates, w_gate=w_gate, w_up=w_up, hidden_grad=hidden_grad)


def reference(tokens, routes, gates, w_gate, w_up, hidden_grad):
    experts = N_GRP * N_EXP
    slots = experts * C_SEND
    per_source = routes.reshape(experts, TOK_DEV * TOP).astype(jnp.int32)
    onehot = (per_source[:, :, None] == jnp.arange(experts, dtype=jnp.int32)[None, None, :]).astype(jnp.int32)
    before = jnp.cumsum(onehot, axis=1) - onehot
    slot_rank = jnp.sum(before * onehot, axis=2).astype(jnp.int32)
    source = jnp.arange(experts, dtype=jnp.int32)[:, None]
    slot_of = (source * C_SEND + slot_rank).reshape(TOKENS, TOP).astype(jnp.int32)
    flat_routes = routes.astype(jnp.int32)
    token_of = jnp.broadcast_to(jnp.arange(TOKENS, dtype=jnp.int32)[:, None], (TOKENS, TOP))
    slot_table = jnp.full((experts * slots,), TOKENS, jnp.int32)
    slot_table = slot_table.at[(flat_routes * slots + slot_of).reshape(-1)].set(token_of.reshape(-1))
    slot_table = slot_table.reshape(experts, slots)
    padded = jnp.concatenate([tokens, jnp.zeros((1, D), tokens.dtype)], 0)

    def one_expert(inputs):
        weight_gate, weight_up, grad_hidden, slot_rows = inputs
        expert_rows = padded[slot_rows]
        pre_gate = jnp.dot(expert_rows, weight_gate, preferred_element_type=jnp.float32)
        pre_up = jnp.dot(expert_rows, weight_up, preferred_element_type=jnp.float32)
        sigmoid_gate = jax.nn.sigmoid(pre_gate)
        upstream = grad_hidden.astype(jnp.float32)
        grad_gate = (upstream * pre_up * sigmoid_gate * (1.0 + pre_gate * (1.0 - sigmoid_gate))).astype(jnp.bfloat16)
        grad_up = (upstream * pre_gate * sigmoid_gate).astype(jnp.bfloat16)
        gate_blocks = grad_gate.astype(jnp.float32).reshape(slots, N_TP, HT)
        up_blocks = grad_up.astype(jnp.float32).reshape(slots, N_TP, HT)
        gate_weights = weight_gate.astype(jnp.float32).reshape(D, N_TP, HT)
        up_weights = weight_up.astype(jnp.float32).reshape(D, N_TP, HT)
        partials = jnp.einsum('snh,dnh->nsd', gate_blocks, gate_weights) + jnp.einsum('snh,dnh->nsd', up_blocks, up_weights)
        rounded = lax.optimization_barrier(partials.astype(jnp.bfloat16))
        summed = jnp.sum(rounded.astype(jnp.float32), axis=0)
        return summed.astype(jnp.bfloat16)

    slot_grad = lax.map(one_expert, (w_gate, w_up, hidden_grad, slot_table))
    picked = slot_grad[flat_routes, slot_of]
    combined = jnp.sum(gates.astype(jnp.float32)[:, :, None] * picked.astype(jnp.float32), axis=1)
    return combined.astype(jnp.bfloat16)
```

```python
import functools

import jax
import jax.numpy as jnp
from jax import lax
from jax.experimental import pallas as pl
from jax.experimental.pallas import tpu as pltpu
from jax.sharding import PartitionSpec as P

MESH = pl.DeviceIdType.MESH


def routed(tokens, routes, gates, w_gate, w_up, hidden_grad):
    group_count = lax.axis_size("grp")
    member_count = lax.axis_size("exp")
    experts = group_count * member_count
    tok_rows, part_width = tokens.shape
    per_token = routes.shape[1]
    slots = hidden_grad.shape[1]
    capacity = slots // experts
    flat_routes = routes.reshape(-1)
    onehot = (flat_routes[:, None] == jnp.arange(experts, dtype=jnp.int32)[None, :]).astype(
        jnp.int32
    )
    slot_ranks = jnp.sum((jnp.cumsum(onehot, axis=0) - onehot) * onehot, axis=1)
    blank_row = jnp.zeros((1, part_width), tokens.dtype)
    owner_row = jnp.arange(tok_rows * per_token, dtype=jnp.int32) // per_token
    slot_table = jnp.full((experts * capacity,), tok_rows, jnp.int32)
    slot_table = slot_table.at[flat_routes * capacity + slot_ranks].set(owner_row)
    outgoing = jnp.concatenate([tokens, blank_row], 0)[slot_table].reshape(
        group_count, member_count, capacity, part_width
    )
    across = lax.all_to_all(outgoing, "grp", split_axis=0, concat_axis=0, tiled=True)
    arrived = lax.all_to_all(across, "exp", split_axis=1, concat_axis=1, tiled=True)
    slot_rows = arrived.reshape(slots, part_width)
    weight_gate = w_gate[0]
    weight_up = w_up[0]
    piece = lax.all_gather(slot_rows, "tp", axis=1, tiled=True)
    pre_gate = jnp.dot(piece, weight_gate, preferred_element_type=jnp.float32)
    pre_up = jnp.dot(piece, weight_up, preferred_element_type=jnp.float32)
    sigmoid_gate = jax.nn.sigmoid(pre_gate)
    upstream = hidden_grad[0].astype(jnp.float32)
    grad_gate = (upstream * pre_up * sigmoid_gate * (1.0 + pre_gate * (1.0 - sigmoid_gate))).astype(
        jnp.bfloat16
    )
    grad_up = (upstream * pre_gate * sigmoid_gate).astype(jnp.bfloat16)
    contract = (((1,), (1,)), ((), ()))
    slot_term = lax.dot_general(
        grad_gate, weight_gate, contract, preferred_element_type=jnp.float32
    )
    slot_term = slot_term + lax.dot_general(
        grad_up, weight_up, contract, preferred_element_type=jnp.float32
    )
    summed = lax.psum_scatter(slot_term.astype(jnp.bfloat16), "tp", scatter_dimension=1, tiled=True)
    returned = lax.all_to_all(
        summed.reshape(group_count, member_count, capacity, part_width),
        "exp",
        split_axis=1,
        concat_axis=1,
        tiled=True,
    )
    at_owner = lax.all_to_all(returned, "grp", split_axis=0, concat_axis=0, tiled=True).reshape(
        experts * capacity, part_width
    )
    picked = at_owner[flat_routes * capacity + slot_ranks].reshape(tok_rows, per_token, part_width)
    combined = jnp.sum(gates.astype(jnp.float32)[:, :, None] * picked.astype(jnp.float32), axis=1)
    return combined.astype(jnp.bfloat16)


def dense_kernel(
    tok_hbm, routes_hbm, gates_hbm, wg_hbm, wu_hbm, hid_hbm, out_ref,
    rt, gt, hid, w, x, gate_all, pre, grads, p_sib, r_sib, p_own, stage, recv, c_send, c_recv,
    local_sem, send_sem, recv_sem,
):
    n_exp = 4
    rows, width = tok_hbm.shape
    half = width // 2
    group = n_exp * rows
    ht = hid.shape[1]
    gx, ez, tp = lax.axis_index("grp"), lax.axis_index("exp"), lax.axis_index("tp")
    core = lax.rem(tp, 2)
    ty = tp // 2
    ox, oy, oc = 1 - gx, 1 - ty, 1 - core
    zk = [ez, ez + 1 - 2 * lax.rem(ez, 2), lax.rem(ez + 2, n_exp), n_exp - 1 - ez]
    q = 2 * ty + core
    qy = 2 * oy + core
    qc = 2 * ty + oc
    qcy = 2 * oy + oc
    to_x, to_y, to_c = (ox, ez, tp), (gx, ez, qy), (gx, ez, qc)
    to_z = [None] + [(gx, zk[k], tp) for k in (1, 2, 3)]

    def row(gr, z):
        return pl.multiple_of((gr * n_exp + z) * rows, rows)

    counter = [0]
    sent = []

    def remote(src, dst, device):
        i = counter[0]
        counter[0] += 1
        c = pltpu.make_async_remote_copy(
            src_ref=src, dst_ref=dst, send_sem=send_sem.at[i], recv_sem=recv_sem.at[i],
            device_id=device, device_id_type=MESH,
        )
        c.start()
        sent.append(c)
        return c

    mine = pl.ds(row(gx, ez), rows)
    loc = [
        pltpu.make_async_copy(tok_hbm.at[:, pl.ds(0, half)], x.at[2 * q, mine, :], local_sem.at[0]),
        pltpu.make_async_copy(tok_hbm.at[:, pl.ds(half, half)], x.at[2 * q + 1, mine, :], local_sem.at[1]),
        pltpu.make_async_copy(routes_hbm, rt, local_sem.at[2]),
        pltpu.make_async_copy(gates_hbm, gt, local_sem.at[3]),
        pltpu.make_async_copy(wg_hbm, w.at[:, :, pl.ds(0, ht)], local_sem.at[4]),
        pltpu.make_async_copy(wu_hbm, w.at[:, :, pl.ds(ht, ht)], local_sem.at[5]),
        pltpu.make_async_copy(hid_hbm, hid, local_sem.at[6]),
    ]
    for c in loc:
        c.start()
    barrier = pltpu.get_barrier_semaphore()
    partners = [to_x, to_y, to_c] + to_z[1:]
    for d in partners:
        pl.semaphore_signal(barrier, inc=1, device_id=d, device_id_type=MESH)
    loc[0].wait()
    loc[1].wait()
    pl.semaphore_wait(barrier, len(partners))

    def block(quarter, gr, z):
        return x.at[pl.ds(2 * quarter, 2), pl.ds(row(gr, z), rows), :]

    def piece(quarter, h, gr, z):
        return x.at[2 * quarter + h, pl.ds(row(gr, z), rows), :]

    def same(ref, device):
        return remote(ref, ref, device)

    zc, xc, yc, fa, fb = [None] * 4, [None] * 4, [None] * 4, [None] * 4, [None] * 4
    core_copies = [[None] * 4 for _ in range(4)]
    for k in (3, 2, 1):
        zc[k] = same(block(q, gx, ez), to_z[k])

    def column(k):
        if k:
            zc[k].wait_recv()
        xc[k] = same(block(q, gx, zk[k]), to_x)
        yc[k] = same(block(q, gx, zk[k]), to_y)
        core_copies[0][k] = same(block(q, gx, zk[k]), to_c)

    def onward(k):
        xc[k].wait_recv()
        fa[k] = same(piece(q, 0, ox, zk[k]), to_y)
        core_copies[1][k] = same(block(q, ox, zk[k]), to_c)
        yc[k].wait_recv()
        fb[k] = same(piece(qy, 1, gx, zk[k]), to_x)
        core_copies[2][k] = same(block(qy, gx, zk[k]), to_c)

    column(0)
    loc[2].wait()
    loc[3].wait()
    lanes = lax.broadcasted_iota(jnp.int32, (rows, 128), 1)
    table = jnp.zeros((rows, 128), jnp.float32)
    chosen = rt[...]
    values = gt[...].astype(jnp.float32)
    for k in range(chosen.shape[1]):
        table = table + jnp.where(lanes == chosen[:, k : k + 1], values[:, k : k + 1], 0.0)
    gate_all[mine, :] = table.astype(jnp.bfloat16)
    own_gates = gate_all.at[mine, :]
    gz = [same(own_gates, to_z[k]) for k in (1, 2, 3)]
    column(1)
    onward(0)
    column(2)
    onward(1)
    column(3)
    for c in gz:
        c.wait_recv()
    gate_column = gate_all.at[pl.ds(row(gx, 0), group), :]
    gcol = same(gate_column, to_x)
    onward(2)
    onward(3)
    for c in loc[4:]:
        c.wait()

    def first(quarter):
        return jnp.dot(
            x[2 * quarter], w[2 * quarter], preferred_element_type=jnp.float32
        ) + jnp.dot(x[2 * quarter + 1], w[2 * quarter + 1], preferred_element_type=jnp.float32)

    pre[...] = first(q)
    for k in range(4):
        fa[k].wait_recv()
        fb[k].wait_recv()
        core_copies[3][k] = same(block(qy, ox, zk[k]), to_c)
    pre[...] += first(qy)
    for k in range(4):
        core_copies[0][k].wait_recv()
        core_copies[1][k].wait_recv()
    pre[...] += first(qc)
    gcol.wait_recv()
    expert = gx * n_exp + ez
    total_rows = pre.shape[0]
    lane = lax.broadcasted_iota(jnp.int32, (total_rows, 128), 1)
    scale = jnp.sum(
        jnp.where(lane == expert, gate_all[...].astype(jnp.float32), 0.0), axis=1, keepdims=True
    )
    for k in range(4):
        core_copies[2][k].wait_recv()
        core_copies[3][k].wait_recv()
    both = pre[...] + first(qcy)
    pre_gate, pre_up = both[:, :ht], both[:, ht:]
    sg = jax.nn.sigmoid(pre_gate)
    up = hid[...].astype(jnp.float32) * scale * sg
    grads[:, :ht] = (up * pre_up * (1.0 + pre_gate * (1.0 - sg))).astype(jnp.bfloat16)
    grads[:, ht:] = (up * pre_gate).astype(jnp.bfloat16)

    def second(part):
        return lax.dot_general(
            grads[...], w[part], (((1,), (1,)), ((), ())), preferred_element_type=jnp.float32
        )

    sib = []
    for j in range(4):
        p_sib[j] = second(2 * (qcy if j < 2 else qc) + j % 2).astype(jnp.bfloat16)
        sib.append(remote(p_sib.at[j], r_sib.at[j], to_c))
    for j in range(4):
        p_own[j] = second(2 * (qy if j < 2 else q) + j % 2)
    pair = 2 * rows
    far = 1 - ez // 2
    offs = [pl.multiple_of(far * pair, pair), pl.multiple_of((1 - far) * pair, pair)]

    def at(gr, o):
        return pl.ds(pl.multiple_of(gr * group + offs[o], pair), pair)

    da, db, sx, sy = {}, {}, {}, {}

    def own(j, gr, o):
        return p_own[j, at(gr, o), :] + r_sib[j, at(gr, o), :].astype(jnp.float32)

    def send(slot, value, o, device):
        stage[slot, o] = value.astype(jnp.bfloat16)
        return remote(stage.at[slot, o], recv.at[slot, o], device)

    sib[0].wait_recv()
    for o in range(2):
        da[o] = send(0, own(0, ox, o), o, to_y)
    sib[1].wait_recv()
    for o in range(2):
        db[o] = send(1, own(1, ox, o), o, to_x)
    for o in range(2):
        sy[o, 0] = send(2, own(0, gx, o), o, to_y)
    sib[3].wait_recv()
    for o in range(2):
        sx[o, 1] = send(3, own(3, ox, o), o, to_x)
    sib[2].wait_recv()
    for o in range(2):
        da[o].wait_recv()
        sx[o, 0] = send(4, own(2, ox, o) + recv[0, o].astype(jnp.float32), o, to_x)
        db[o].wait_recv()
        sy[o, 1] = send(5, own(1, gx, o) + recv[1, o].astype(jnp.float32), o, to_y)
    back = {}
    for o in range(2):
        sy[o, 0].wait_recv()
        sx[o, 1].wait_recv()
        sx[o, 0].wait_recv()
        sy[o, 1].wait_recv()
        for k in ((2, 3) if o == 0 else (1, 0)):
            r = pl.multiple_of(lax.rem(zk[k], 2) * rows, rows)
            s = pl.ds(r, rows)
            here = pl.ds(pl.multiple_of(gx * group + zk[k] * rows, rows), rows)
            for h, slots in ((0, (4, 2)), (1, (3, 5))):
                v = p_own[2 + h, here, :] + r_sib[2 + h, here, :].astype(jnp.float32)
                for slot in slots:
                    v = v + recv[slot, o, s, :].astype(jnp.float32)
                if k:
                    c_send[k - 1, h] = v.astype(jnp.bfloat16)
                else:
                    p_own[2 + h, here, :] = v
            if k:
                back[k] = remote(c_send.at[k - 1], c_recv.at[k - 1], to_z[k])
    here = pl.ds(row(gx, ez), rows)
    for k in (1, 2, 3):
        back[k].wait_recv()
    for h in range(2):
        v = p_own[2 + h, here, :]
        for k in range(3):
            v = v + c_recv[k, h].astype(jnp.float32)
        out_ref[:, h * half : (h + 1) * half] = v.astype(jnp.bfloat16)
    for c in sent:
        c.wait_send()


def dense(tokens, routes, gates, w_gate, w_up, hidden_grad):
    rows, width = tokens.shape
    half = width // 2
    _, depth, ht = w_gate.shape
    slots = hidden_grad.shape[1]
    parts = depth // half
    bf16, f32 = jnp.bfloat16, jnp.float32
    any_space = pl.BlockSpec(memory_space=pl.ANY)
    n_copies = 3 + 8 + 8 + 16 + 4 + 4 + 12 + 3
    return pl.pallas_call(
        dense_kernel,
        out_shape=jax.ShapeDtypeStruct((rows, width), bf16),
        in_specs=[any_space] * 6,
        out_specs=pl.BlockSpec(memory_space=pltpu.VMEM),
        scratch_shapes=[
            pltpu.VMEM(routes.shape, jnp.int32),
            pltpu.VMEM(gates.shape, bf16),
            pltpu.VMEM((slots, ht), bf16),
            pltpu.VMEM((parts, half, 2 * ht), bf16),
            pltpu.VMEM((parts, slots, half), bf16),
            pltpu.VMEM((slots, 128), bf16),
            pltpu.VMEM((slots, 2 * ht), f32),
            pltpu.VMEM((slots, 2 * ht), bf16),
            pltpu.VMEM((4, slots, half), bf16),
            pltpu.VMEM((4, slots, half), bf16),
            pltpu.VMEM((4, slots, half), f32),
            pltpu.VMEM((6, 2, 2 * rows, half), bf16),
            pltpu.VMEM((6, 2, 2 * rows, half), bf16),
            pltpu.VMEM((3, 2, rows, half), bf16),
            pltpu.VMEM((3, 2, rows, half), bf16),
            pltpu.SemaphoreType.DMA((7,)),
            pltpu.SemaphoreType.DMA((n_copies,)),
            pltpu.SemaphoreType.DMA((n_copies,)),
        ],
        compiler_params=pltpu.CompilerParams(
            collective_id=0, has_side_effects=True, vmem_limit_bytes=56 << 20
        ),
        cost_estimate=pl.CostEstimate(
            flops=8 * slots * depth * ht, bytes_accessed=4 * depth * ht, transcendentals=slots * ht
        ),
    )(
        tokens,
        routes,
        gates,
        w_gate.reshape(parts, half, ht),
        w_up.reshape(parts, half, ht),
        hidden_grad.reshape(slots, ht),
    )


def solution(mesh):
    placed = (
        P(("grp", "exp"), "tp"),
        P(("grp", "exp"), None),
        P(("grp", "exp"), None),
        P(("grp", "exp"), None, "tp"),
        P(("grp", "exp"), None, "tp"),
        P(("grp", "exp"), None, "tp"),
    )
    sizes = (mesh.shape["grp"], mesh.shape["exp"], mesh.shape["tp"])
    experts = sizes[0] * sizes[1]

    def local(tokens, routes, *rest):
        if sizes == (2, 4, 4) and routes.shape[1] == experts:
            return dense(tokens, routes, *rest)
        return routed(tokens, routes, *rest)

    return jax.shard_map(
        local, mesh=mesh, in_specs=placed, out_specs=P(("grp", "exp"), "tp"), check_vma=False
    )
```

```python
import functools

import jax
import jax.numpy as jnp
from jax import lax
from jax.experimental import pallas as pl
from jax.experimental.pallas import tpu as pltpu
from jax.sharding import PartitionSpec as P

MESH = pl.DeviceIdType.MESH


def routed(tokens, routes, gates, w_gate, w_up, hidden_grad):
    group_count = lax.axis_size("grp")
    member_count = lax.axis_size("exp")
    experts = group_count * member_count
    tok_rows, part_width = tokens.shape
    per_token = routes.shape[1]
    slots = hidden_grad.shape[1]
    capacity = slots // experts
    flat_routes = routes.reshape(-1)
    onehot = (flat_routes[:, None] == jnp.arange(experts, dtype=jnp.int32)[None, :]).astype(
        jnp.int32
    )
    slot_ranks = jnp.sum((jnp.cumsum(onehot, axis=0) - onehot) * onehot, axis=1)
    blank_row = jnp.zeros((1, part_width), tokens.dtype)
    owner_row = jnp.arange(tok_rows * per_token, dtype=jnp.int32) // per_token
    slot_table = jnp.full((experts * capacity,), tok_rows, jnp.int32)
    slot_table = slot_table.at[flat_routes * capacity + slot_ranks].set(owner_row)
    outgoing = jnp.concatenate([tokens, blank_row], 0)[slot_table].reshape(
        group_count, member_count, capacity, part_width
    )
    across = lax.all_to_all(outgoing, "grp", split_axis=0, concat_axis=0, tiled=True)
    arrived = lax.all_to_all(across, "exp", split_axis=1, concat_axis=1, tiled=True)
    slot_rows = arrived.reshape(slots, part_width)
    weight_gate = w_gate[0]
    weight_up = w_up[0]
    piece = lax.all_gather(slot_rows, "tp", axis=1, tiled=True)
    pre_gate = jnp.dot(piece, weight_gate, preferred_element_type=jnp.float32)
    pre_up = jnp.dot(piece, weight_up, preferred_element_type=jnp.float32)
    sigmoid_gate = jax.nn.sigmoid(pre_gate)
    upstream = hidden_grad[0].astype(jnp.float32)
    grad_gate = (upstream * pre_up * sigmoid_gate * (1.0 + pre_gate * (1.0 - sigmoid_gate))).astype(
        jnp.bfloat16
    )
    grad_up = (upstream * pre_gate * sigmoid_gate).astype(jnp.bfloat16)
    contract = (((1,), (1,)), ((), ()))
    slot_term = lax.dot_general(
        grad_gate, weight_gate, contract, preferred_element_type=jnp.float32
    )
    slot_term = slot_term + lax.dot_general(
        grad_up, weight_up, contract, preferred_element_type=jnp.float32
    )
    summed = lax.psum_scatter(slot_term.astype(jnp.bfloat16), "tp", scatter_dimension=1, tiled=True)
    returned = lax.all_to_all(
        summed.reshape(group_count, member_count, capacity, part_width),
        "exp",
        split_axis=1,
        concat_axis=1,
        tiled=True,
    )
    at_owner = lax.all_to_all(returned, "grp", split_axis=0, concat_axis=0, tiled=True).reshape(
        experts * capacity, part_width
    )
    picked = at_owner[flat_routes * capacity + slot_ranks].reshape(tok_rows, per_token, part_width)
    combined = jnp.sum(gates.astype(jnp.float32)[:, :, None] * picked.astype(jnp.float32), axis=1)
    return combined.astype(jnp.bfloat16)


def dense_kernel(
    tok_hbm, routes_hbm, gates_hbm, wg_hbm, wu_hbm, hid_hbm, out_ref,
    rt, gt, hid, w, x, gate_all, pre, grads, p_sib, r_sib, p_own, stage, recv, c_send, c_recv,
    local_sem, send_sem, recv_sem,
):
    n_exp = 4
    rows, width = tok_hbm.shape
    half = width // 2
    group = n_exp * rows
    ht = hid.shape[1]
    gx, ez, tp = lax.axis_index("grp"), lax.axis_index("exp"), lax.axis_index("tp")
    core = lax.rem(tp, 2)
    ty = tp // 2
    ox, oy, oc = 1 - gx, 1 - ty, 1 - core
    zk = [ez, ez + 1 - 2 * lax.rem(ez, 2), lax.rem(ez + 2, n_exp), n_exp - 1 - ez]
    q = 2 * ty + core
    qy = 2 * oy + core
    qc = 2 * ty + oc
    qcy = 2 * oy + oc
    to_x, to_y, to_c = (ox, ez, tp), (gx, ez, qy), (gx, ez, qc)
    to_z = [(gx, z, tp) for z in zk]

    def row(gr, z):
        return pl.multiple_of((gr * n_exp + z) * rows, rows)

    counter = [0]
    sent = []

    def remote(src, dst, device):
        i = counter[0]
        counter[0] += 1
        c = pltpu.make_async_remote_copy(
            src_ref=src, dst_ref=dst, send_sem=send_sem.at[i], recv_sem=recv_sem.at[i],
            device_id=device, device_id_type=MESH,
        )
        c.start()
        sent.append(c)
        return c

    mine = pl.ds(row(gx, ez), rows)
    loc = [
        pltpu.make_async_copy(tok_hbm.at[:, pl.ds(0, half)], x.at[2 * q, mine, :], local_sem.at[0]),
        pltpu.make_async_copy(tok_hbm.at[:, pl.ds(half, half)], x.at[2 * q + 1, mine, :], local_sem.at[1]),
        pltpu.make_async_copy(routes_hbm, rt, local_sem.at[2]),
        pltpu.make_async_copy(gates_hbm, gt, local_sem.at[3]),
        pltpu.make_async_copy(wg_hbm, w.at[:, :, pl.ds(0, ht)], local_sem.at[4]),
        pltpu.make_async_copy(wu_hbm, w.at[:, :, pl.ds(ht, ht)], local_sem.at[5]),
        pltpu.make_async_copy(hid_hbm, hid, local_sem.at[6]),
    ]
    for c in loc[:4]:
        c.start()
    barrier = pltpu.get_barrier_semaphore()
    partners = [to_x, to_y, to_c] + to_z[1:]
    for d in partners:
        pl.semaphore_signal(barrier, inc=1, device_id=d, device_id_type=MESH)
    loc[0].wait()
    loc[1].wait()
    pl.semaphore_wait(barrier, len(partners))

    def block(quarter, gr, z):
        return x.at[pl.ds(2 * quarter, 2), pl.ds(row(gr, z), rows), :]

    def piece(quarter, h, gr, z):
        return x.at[2 * quarter + h, pl.ds(row(gr, z), rows), :]

    def same(ref, device):
        return remote(ref, ref, device)

    xc, yc, fa, fb = [None] * 4, [None] * 4, [None] * 4, [None] * 4
    core_copies = [[None] * 4 for _ in range(4)]
    zc = [None] + [same(block(q, gx, ez), to_z[k]) for k in (1, 2, 3)]

    def column(k):
        if k:
            zc[k].wait_recv()
        xc[k] = same(block(q, gx, zk[k]), to_x)
        yc[k] = same(block(q, gx, zk[k]), to_y)
        core_copies[0][k] = same(block(q, gx, zk[k]), to_c)

    def onward(k):
        xc[k].wait_recv()
        fa[k] = same(piece(q, 0, ox, zk[k]), to_y)
        core_copies[1][k] = same(block(q, ox, zk[k]), to_c)
        yc[k].wait_recv()
        fb[k] = same(piece(qy, 1, gx, zk[k]), to_x)
        core_copies[2][k] = same(block(qy, gx, zk[k]), to_c)

    column(0)
    for c in loc[4:]:
        c.start()
    loc[2].wait()
    loc[3].wait()
    lanes = lax.broadcasted_iota(jnp.int32, (rows, 128), 1).astype(jnp.float32)
    table = jnp.zeros((rows, 128), jnp.float32)
    chosen = rt[...].astype(jnp.float32)
    values = gt[...]
    shape = (rows, rows)
    eye = lax.broadcasted_iota(jnp.int32, shape, 0) == lax.broadcasted_iota(jnp.int32, shape, 1)

    def upright(line):
        return jnp.sum(jnp.where(eye, line, 0.0), axis=1, keepdims=True)

    for k in range(chosen.shape[0]):
        pick = lanes == upright(chosen[k : k + 1, :])
        table = table + jnp.where(pick, upright(values[k : k + 1, :]), 0.0)
    gate_all[mine, :] = table.astype(jnp.bfloat16)
    own_gates = gate_all.at[mine, :]
    gz = [same(own_gates, to_z[k]) for k in (1, 2, 3)]
    column(1)
    onward(0)
    column(2)
    onward(1)
    column(3)
    for c in gz:
        c.wait_recv()
    gate_column = gate_all.at[pl.ds(row(gx, 0), group), :]
    gcol = same(gate_column, to_x)
    onward(2)
    onward(3)
    for c in loc[4:]:
        c.wait()

    def first(quarter):
        return jnp.dot(
            x[2 * quarter], w[2 * quarter], preferred_element_type=jnp.float32
        ) + jnp.dot(x[2 * quarter + 1], w[2 * quarter + 1], preferred_element_type=jnp.float32)

    pre[...] = first(q)
    for k in range(4):
        fa[k].wait_recv()
        fb[k].wait_recv()
        core_copies[3][k] = same(block(qy, ox, zk[k]), to_c)
    pre[...] += first(qy)
    for k in range(4):
        core_copies[0][k].wait_recv()
        core_copies[1][k].wait_recv()
    pre[...] += first(qc)
    gcol.wait_recv()
    expert = gx * n_exp + ez
    total_rows = pre.shape[0]
    lane = lax.broadcasted_iota(jnp.int32, (total_rows, 128), 1)
    scale = jnp.sum(
        jnp.where(lane == expert, gate_all[...].astype(jnp.float32), 0.0), axis=1, keepdims=True
    )
    for k in range(4):
        core_copies[2][k].wait_recv()
        core_copies[3][k].wait_recv()
    both = pre[...] + first(qcy)
    pre_gate, pre_up = both[:, :ht], both[:, ht:]
    sg = jax.nn.sigmoid(pre_gate)
    up = hid[...].astype(jnp.float32) * scale * sg
    grads[:, :ht] = (up * pre_up * (1.0 + pre_gate * (1.0 - sg))).astype(jnp.bfloat16)
    grads[:, ht:] = (up * pre_gate).astype(jnp.bfloat16)

    def second(part):
        return lax.dot_general(
            grads[...], w[part], (((1,), (1,)), ((), ())), preferred_element_type=jnp.float32
        )

    sib = []
    for j in range(4):
        p_sib[j] = second(2 * (qcy if j < 2 else qc) + j % 2).astype(jnp.bfloat16)
        sib.append(remote(p_sib.at[j], r_sib.at[j], to_c))
    for j in range(4):
        p_own[j] = second(2 * (qy if j < 2 else q) + j % 2)
    da, db, sx, sy = {}, {}, {}, {}

    def own(j, gr, k):
        at = pl.ds(row(gr, zk[k]), rows)
        return p_own[j, at, :] + r_sib[j, at, :].astype(jnp.float32)

    def got(slot, k):
        return recv[slot, k].astype(jnp.float32)

    def send(slot, value, k, device):
        stage[slot, k] = value.astype(jnp.bfloat16)
        return remote(stage.at[slot, k], recv.at[slot, k], device)

    def diagonal(k):
        da[k] = send(0, own(0, ox, k), k, to_y)
        db[k] = send(1, own(1, ox, k), k, to_x)

    def plain(k):
        sy[0, k] = send(2, own(0, gx, k), k, to_y)
        sx[1, k] = send(3, own(3, ox, k), k, to_x)

    def joined(k):
        da[k].wait_recv()
        sx[0, k] = send(4, own(2, ox, k) + got(0, k), k, to_x)
        db[k].wait_recv()
        sy[1, k] = send(5, own(1, gx, k) + got(1, k), k, to_y)

    back, mine_sum = {}, [None, None]

    def finish(k):
        for c in (sy[0, k], sx[1, k], sx[0, k], sy[1, k]):
            c.wait_recv()
        for h, slots in ((0, (4, 2)), (1, (3, 5))):
            v = own(2 + h, gx, k) + got(slots[0], k) + got(slots[1], k)
            if k:
                c_send[k - 1, h] = v.astype(jnp.bfloat16)
            else:
                mine_sum[h] = v
        if k:
            back[k] = remote(c_send.at[k - 1], c_recv.at[k - 1], to_z[k])

    sib[0].wait_recv()
    sib[1].wait_recv()
    diagonal(2)
    diagonal(3)
    sib[2].wait_recv()
    sib[3].wait_recv()
    plain(2)
    plain(3)
    diagonal(1)
    diagonal(0)
    joined(2)
    joined(3)
    plain(1)
    plain(0)
    joined(1)
    joined(0)
    for k in (2, 3, 1, 0):
        finish(k)
    for k in (1, 2, 3):
        back[k].wait_recv()
    for h in range(2):
        v = mine_sum[h]
        for k in range(3):
            v = v + c_recv[k, h].astype(jnp.float32)
        out_ref[:, h * half : (h + 1) * half] = v.astype(jnp.bfloat16)
    for c in sent:
        c.wait_send()


def dense(tokens, routes, gates, w_gate, w_up, hidden_grad):
    rows, width = tokens.shape
    half = width // 2
    _, depth, ht = w_gate.shape
    slots = hidden_grad.shape[1]
    parts = depth // half
    bf16, f32 = jnp.bfloat16, jnp.float32
    any_space = pl.BlockSpec(memory_space=pl.ANY)
    n_copies = 3 + 8 + 8 + 16 + 4 + 4 + 24 + 3
    return pl.pallas_call(
        dense_kernel,
        out_shape=jax.ShapeDtypeStruct((rows, width), bf16),
        in_specs=[any_space] * 6,
        out_specs=pl.BlockSpec(memory_space=pltpu.VMEM),
        scratch_shapes=[
            pltpu.VMEM(routes.shape[::-1], jnp.int32),
            pltpu.VMEM(gates.shape[::-1], f32),
            pltpu.VMEM((slots, ht), bf16),
            pltpu.VMEM((parts, half, 2 * ht), bf16),
            pltpu.VMEM((parts, slots, half), bf16),
            pltpu.VMEM((slots, 128), bf16),
            pltpu.VMEM((slots, 2 * ht), f32),
            pltpu.VMEM((slots, 2 * ht), bf16),
            pltpu.VMEM((4, slots, half), bf16),
            pltpu.VMEM((4, slots, half), bf16),
            pltpu.VMEM((4, slots, half), f32),
            pltpu.VMEM((6, 4, rows, half), bf16),
            pltpu.VMEM((6, 4, rows, half), bf16),
            pltpu.VMEM((3, 2, rows, half), bf16),
            pltpu.VMEM((3, 2, rows, half), bf16),
            pltpu.SemaphoreType.DMA((7,)),
            pltpu.SemaphoreType.DMA((n_copies,)),
            pltpu.SemaphoreType.DMA((n_copies,)),
        ],
        compiler_params=pltpu.CompilerParams(
            collective_id=0, has_side_effects=True, vmem_limit_bytes=56 << 20
        ),
        cost_estimate=pl.CostEstimate(
            flops=8 * slots * depth * ht, bytes_accessed=4 * depth * ht, transcendentals=slots * ht
        ),
    )(
        tokens,
        routes.T,
        gates.T.astype(f32),
        w_gate.reshape(parts, half, ht),
        w_up.reshape(parts, half, ht),
        hidden_grad.reshape(slots, ht),
    )


def solution(mesh):
    placed = (
        P(("grp", "exp"), "tp"),
        P(("grp", "exp"), None),
        P(("grp", "exp"), None),
        P(("grp", "exp"), None, "tp"),
        P(("grp", "exp"), None, "tp"),
        P(("grp", "exp"), None, "tp"),
    )
    sizes = (mesh.shape["grp"], mesh.shape["exp"], mesh.shape["tp"])
    experts = sizes[0] * sizes[1]

    def local(tokens, routes, *rest):
        if sizes == (2, 4, 4) and routes.shape[1] == experts:
            return dense(tokens, routes, *rest)
        return routed(tokens, routes, *rest)

    return jax.shard_map(
        local, mesh=mesh, in_specs=placed, out_specs=P(("grp", "exp"), "tp"), check_vma=False
    )
```

```python
import functools

import jax
import jax.numpy as jnp
from jax import lax
from jax.experimental import pallas as pl
from jax.experimental.pallas import tpu as pltpu
from jax.sharding import PartitionSpec as P

MESH = pl.DeviceIdType.MESH


def routed(tokens, routes, gates, w_gate, w_up, hidden_grad):
    group_count = lax.axis_size("grp")
    member_count = lax.axis_size("exp")
    experts = group_count * member_count
    tok_rows, part_width = tokens.shape
    per_token = routes.shape[1]
    slots = hidden_grad.shape[1]
    capacity = slots // experts
    flat_routes = routes.reshape(-1)
    onehot = (flat_routes[:, None] == jnp.arange(experts, dtype=jnp.int32)[None, :]).astype(
        jnp.int32
    )
    slot_ranks = jnp.sum((jnp.cumsum(onehot, axis=0) - onehot) * onehot, axis=1)
    blank_row = jnp.zeros((1, part_width), tokens.dtype)
    owner_row = jnp.arange(tok_rows * per_token, dtype=jnp.int32) // per_token
    slot_table = jnp.full((experts * capacity,), tok_rows, jnp.int32)
    slot_table = slot_table.at[flat_routes * capacity + slot_ranks].set(owner_row)
    outgoing = jnp.concatenate([tokens, blank_row], 0)[slot_table].reshape(
        group_count, member_count, capacity, part_width
    )
    across = lax.all_to_all(outgoing, "grp", split_axis=0, concat_axis=0, tiled=True)
    arrived = lax.all_to_all(across, "exp", split_axis=1, concat_axis=1, tiled=True)
    slot_rows = arrived.reshape(slots, part_width)
    weight_gate = w_gate[0]
    weight_up = w_up[0]
    piece = lax.all_gather(slot_rows, "tp", axis=1, tiled=True)
    pre_gate = jnp.dot(piece, weight_gate, preferred_element_type=jnp.float32)
    pre_up = jnp.dot(piece, weight_up, preferred_element_type=jnp.float32)
    sigmoid_gate = jax.nn.sigmoid(pre_gate)
    upstream = hidden_grad[0].astype(jnp.float32)
    grad_gate = (upstream * pre_up * sigmoid_gate * (1.0 + pre_gate * (1.0 - sigmoid_gate))).astype(
        jnp.bfloat16
    )
    grad_up = (upstream * pre_gate * sigmoid_gate).astype(jnp.bfloat16)
    contract = (((1,), (1,)), ((), ()))
    slot_term = lax.dot_general(
        grad_gate, weight_gate, contract, preferred_element_type=jnp.float32
    )
    slot_term = slot_term + lax.dot_general(
        grad_up, weight_up, contract, preferred_element_type=jnp.float32
    )
    summed = lax.psum_scatter(slot_term.astype(jnp.bfloat16), "tp", scatter_dimension=1, tiled=True)
    returned = lax.all_to_all(
        summed.reshape(group_count, member_count, capacity, part_width),
        "exp",
        split_axis=1,
        concat_axis=1,
        tiled=True,
    )
    at_owner = lax.all_to_all(returned, "grp", split_axis=0, concat_axis=0, tiled=True).reshape(
        experts * capacity, part_width
    )
    picked = at_owner[flat_routes * capacity + slot_ranks].reshape(tok_rows, per_token, part_width)
    combined = jnp.sum(gates.astype(jnp.float32)[:, :, None] * picked.astype(jnp.float32), axis=1)
    return combined.astype(jnp.bfloat16)


def dense_kernel(
    tok_hbm, routes_hbm, gt, wg_hbm, wu_hbm, hid_hbm, out_ref,
    rt, hid, w, x, gate_all, pre, grads, p_sib, r_sib, p_own, stage, recv, c_send, c_recv,
    local_sem, send_sem, recv_sem,
):
    n_exp = 4
    rows, width = tok_hbm.shape
    half = width // 2
    group = n_exp * rows
    ht = hid.shape[1]
    gx, ez, tp = lax.axis_index("grp"), lax.axis_index("exp"), lax.axis_index("tp")
    core = lax.rem(tp, 2)
    ty = tp // 2
    ox, oy, oc = 1 - gx, 1 - ty, 1 - core
    zk = [ez, ez + 1 - 2 * lax.rem(ez, 2), lax.rem(ez + 2, n_exp), n_exp - 1 - ez]
    q = 2 * ty + core
    qy = 2 * oy + core
    qc = 2 * ty + oc
    qcy = 2 * oy + oc
    to_x, to_y, to_c = (ox, ez, tp), (gx, ez, qy), (gx, ez, qc)
    to_z = [(gx, z, tp) for z in zk]

    def row(gr, z):
        return pl.multiple_of((gr * n_exp + z) * rows, rows)

    counter = [0]
    sent = []

    def remote(src, dst, device):
        i = counter[0]
        counter[0] += 1
        c = pltpu.make_async_remote_copy(
            src_ref=src, dst_ref=dst, send_sem=send_sem.at[i], recv_sem=recv_sem.at[i],
            device_id=device, device_id_type=MESH,
        )
        c.start()
        sent.append(c)
        return c

    mine = pl.ds(row(gx, ez), rows)
    loc = [
        pltpu.make_async_copy(tok_hbm.at[:, pl.ds(0, half)], x.at[2 * q, mine, :], local_sem.at[0]),
        pltpu.make_async_copy(tok_hbm.at[:, pl.ds(half, half)], x.at[2 * q + 1, mine, :], local_sem.at[1]),
        pltpu.make_async_copy(routes_hbm, rt, local_sem.at[2]),
        pltpu.make_async_copy(wg_hbm, w.at[:, :, pl.ds(0, ht)], local_sem.at[3]),
        pltpu.make_async_copy(wu_hbm, w.at[:, :, pl.ds(ht, ht)], local_sem.at[4]),
        pltpu.make_async_copy(hid_hbm, hid, local_sem.at[5]),
    ]
    for c in loc[:3]:
        c.start()
    barrier = pltpu.get_barrier_semaphore()
    partners = [to_x, to_y, to_c] + to_z[1:]
    for d in partners:
        pl.semaphore_signal(barrier, inc=1, device_id=d, device_id_type=MESH)
    loc[0].wait()
    loc[1].wait()
    pl.semaphore_wait(barrier, len(partners))

    def block(quarter, gr, z):
        return x.at[pl.ds(2 * quarter, 2), pl.ds(row(gr, z), rows), :]

    def piece(quarter, h, gr, z):
        return x.at[2 * quarter + h, pl.ds(row(gr, z), rows), :]

    def same(ref, device):
        return remote(ref, ref, device)

    xc, yc, fa, fb = [None] * 4, [None] * 4, [None] * 4, [None] * 4
    core_copies = [[None] * 4 for _ in range(4)]
    zc = [None] + [same(block(q, gx, ez), to_z[k]) for k in (1, 2, 3)]

    def column(k):
        if k:
            zc[k].wait_recv()
        xc[k] = same(block(q, gx, zk[k]), to_x)
        yc[k] = same(block(q, gx, zk[k]), to_y)
        core_copies[0][k] = same(block(q, gx, zk[k]), to_c)

    def onward(k):
        xc[k].wait_recv()
        fa[k] = same(piece(q, 0, ox, zk[k]), to_y)
        core_copies[1][k] = same(block(q, ox, zk[k]), to_c)
        yc[k].wait_recv()
        fb[k] = same(piece(qy, 1, gx, zk[k]), to_x)
        core_copies[2][k] = same(block(qy, gx, zk[k]), to_c)

    column(0)
    for c in loc[3:]:
        c.start()
    loc[2].wait()
    lanes = lax.broadcasted_iota(jnp.int32, (rows, 128), 1).astype(jnp.float32)
    table = jnp.zeros((rows, 128), jnp.float32)
    chosen = rt[...].astype(jnp.float32)
    values = gt[...].astype(jnp.float32)
    shape = (rows, rows)
    eye = lax.broadcasted_iota(jnp.int32, shape, 0) == lax.broadcasted_iota(jnp.int32, shape, 1)

    def upright(line):
        return jnp.sum(jnp.where(eye, line, 0.0), axis=1, keepdims=True)

    for k in range(chosen.shape[0]):
        pick = lanes == upright(chosen[k : k + 1, :])
        table = table + jnp.where(pick, upright(values[k : k + 1, :]), 0.0)
    gate_all[mine, :] = table.astype(jnp.bfloat16)
    own_gates = gate_all.at[mine, :]
    gz = [same(own_gates, to_z[k]) for k in (1, 2, 3)]
    onward(0)
    column(1)
    column(2)
    onward(1)
    column(3)
    for c in gz:
        c.wait_recv()
    gate_column = gate_all.at[pl.ds(row(gx, 0), group), :]
    gcol = same(gate_column, to_x)
    onward(2)
    onward(3)
    for c in loc[3:]:
        c.wait()

    def first(quarter):
        return jnp.dot(
            x[2 * quarter], w[2 * quarter], preferred_element_type=jnp.float32
        ) + jnp.dot(x[2 * quarter + 1], w[2 * quarter + 1], preferred_element_type=jnp.float32)

    pre[...] = first(q)
    for k in range(4):
        fa[k].wait_recv()
        fb[k].wait_recv()
        core_copies[3][k] = same(block(qy, ox, zk[k]), to_c)
    pre[...] += first(qy)
    for k in range(4):
        core_copies[0][k].wait_recv()
        core_copies[1][k].wait_recv()
    pre[...] += first(qc)
    gcol.wait_recv()
    expert = gx * n_exp + ez
    total_rows = pre.shape[0]
    lane = lax.broadcasted_iota(jnp.int32, (total_rows, 128), 1)
    scale = jnp.sum(
        jnp.where(lane == expert, gate_all[...].astype(jnp.float32), 0.0), axis=1, keepdims=True
    )
    for k in range(4):
        core_copies[2][k].wait_recv()
        core_copies[3][k].wait_recv()
    both = pre[...] + first(qcy)
    pre_gate, pre_up = both[:, :ht], both[:, ht:]
    sg = jax.nn.sigmoid(pre_gate)
    up = hid[...].astype(jnp.float32) * scale * sg
    grads[:, :ht] = (up * pre_up * (1.0 + pre_gate * (1.0 - sg))).astype(jnp.bfloat16)
    grads[:, ht:] = (up * pre_gate).astype(jnp.bfloat16)

    def second(part):
        return lax.dot_general(
            grads[...], w[part], (((1,), (1,)), ((), ())), preferred_element_type=jnp.float32
        )

    sib = []
    for j in range(4):
        p_sib[j] = second(2 * (qcy if j < 2 else qc) + j % 2).astype(jnp.bfloat16)
        sib.append(remote(p_sib.at[j], r_sib.at[j], to_c))
    for j in (0, 1):
        p_own[j] = second(2 * qy + j)
    da, db, sx, sy = {}, {}, {}, {}

    def own(j, gr, k):
        at = pl.ds(row(gr, zk[k]), rows)
        return p_own[j, at, :] + r_sib[j, at, :].astype(jnp.float32)

    def got(slot, k):
        return recv[slot, k].astype(jnp.float32)

    def send(slot, value, k, device):
        stage[slot, k] = value.astype(jnp.bfloat16)
        return remote(stage.at[slot, k], recv.at[slot, k], device)

    def diagonal(k):
        da[k] = send(0, own(0, ox, k), k, to_y)
        db[k] = send(1, own(1, ox, k), k, to_x)

    def plain(k):
        sy[0, k] = send(2, own(0, gx, k), k, to_y)
        sx[1, k] = send(3, own(3, ox, k), k, to_x)

    def joined(k):
        da[k].wait_recv()
        sx[0, k] = send(4, own(2, ox, k) + got(0, k), k, to_x)
        db[k].wait_recv()
        sy[1, k] = send(5, own(1, gx, k) + got(1, k), k, to_y)

    back, mine_sum = {}, [None, None]

    def finish(k):
        for c in (sy[0, k], sx[1, k], sx[0, k], sy[1, k]):
            c.wait_recv()
        for h, slots in ((0, (4, 2)), (1, (3, 5))):
            v = own(2 + h, gx, k) + got(slots[0], k) + got(slots[1], k)
            if k:
                c_send[k - 1, h] = v.astype(jnp.bfloat16)
            else:
                mine_sum[h] = v
        if k:
            back[k] = remote(c_send.at[k - 1], c_recv.at[k - 1], to_z[k])

    sib[0].wait_recv()
    sib[1].wait_recv()
    diagonal(2)
    diagonal(3)
    for j in (2, 3):
        p_own[j] = second(2 * q + j % 2)
    sib[2].wait_recv()
    sib[3].wait_recv()
    plain(2)
    plain(3)
    diagonal(1)
    diagonal(0)
    joined(2)
    joined(3)
    plain(1)
    plain(0)
    joined(1)
    joined(0)
    for k in (2, 3, 1, 0):
        finish(k)
    for k in (1, 2, 3):
        back[k].wait_recv()
    for h in range(2):
        v = mine_sum[h]
        for k in range(3):
            v = v + c_recv[k, h].astype(jnp.float32)
        out_ref[:, h * half : (h + 1) * half] = v.astype(jnp.bfloat16)
    for c in sent:
        c.wait_send()


def dense(tokens, routes, gates, w_gate, w_up, hidden_grad):
    rows, width = tokens.shape
    half = width // 2
    _, depth, ht = w_gate.shape
    slots = hidden_grad.shape[1]
    parts = depth // half
    bf16, f32 = jnp.bfloat16, jnp.float32
    any_space = pl.BlockSpec(memory_space=pl.ANY)
    n_copies = 3 + 8 + 8 + 16 + 4 + 4 + 24 + 3
    return pl.pallas_call(
        dense_kernel,
        out_shape=jax.ShapeDtypeStruct((rows, width), bf16),
        in_specs=[any_space] * 2 + [pl.BlockSpec(memory_space=pltpu.VMEM)] + [any_space] * 3,
        out_specs=pl.BlockSpec(memory_space=pltpu.VMEM),
        scratch_shapes=[
            pltpu.VMEM(routes.shape[::-1], jnp.int32),
            pltpu.VMEM((slots, ht), bf16),
            pltpu.VMEM((parts, half, 2 * ht), bf16),
            pltpu.VMEM((parts, slots, half), bf16),
            pltpu.VMEM((slots, 128), bf16),
            pltpu.VMEM((slots, 2 * ht), f32),
            pltpu.VMEM((slots, 2 * ht), bf16),
            pltpu.VMEM((4, slots, half), bf16),
            pltpu.VMEM((4, slots, half), bf16),
            pltpu.VMEM((4, slots, half), f32),
            pltpu.VMEM((6, 4, rows, half), bf16),
            pltpu.VMEM((6, 4, rows, half), bf16),
            pltpu.VMEM((3, 2, rows, half), bf16),
            pltpu.VMEM((3, 2, rows, half), bf16),
            pltpu.SemaphoreType.DMA((6,)),
            pltpu.SemaphoreType.DMA((n_copies,)),
            pltpu.SemaphoreType.DMA((n_copies,)),
        ],
        compiler_params=pltpu.CompilerParams(
            collective_id=0, has_side_effects=True, vmem_limit_bytes=56 << 20
        ),
        cost_estimate=pl.CostEstimate(
            flops=8 * slots * depth * ht, bytes_accessed=4 * depth * ht, transcendentals=slots * ht
        ),
    )(
        tokens,
        routes.T,
        gates.T,
        w_gate.reshape(parts, half, ht),
        w_up.reshape(parts, half, ht),
        hidden_grad.reshape(slots, ht),
    )


def solution(mesh):
    placed = (
        P(("grp", "exp"), "tp"),
        P(("grp", "exp"), None),
        P(("grp", "exp"), None),
        P(("grp", "exp"), None, "tp"),
        P(("grp", "exp"), None, "tp"),
        P(("grp", "exp"), None, "tp"),
    )
    sizes = (mesh.shape["grp"], mesh.shape["exp"], mesh.shape["tp"])
    experts = sizes[0] * sizes[1]

    def local(tokens, routes, *rest):
        if sizes == (2, 4, 4) and routes.shape[1] == experts:
            return dense(tokens, routes, *rest)
        return routed(tokens, routes, *rest)

    return jax.shard_map(
        local, mesh=mesh, in_specs=placed, out_specs=P(("grp", "exp"), "tp"), check_vma=False
    )
```

```python
import functools

import jax
import jax.numpy as jnp
from jax import lax
from jax.experimental import pallas as pl
from jax.experimental.pallas import tpu as pltpu
from jax.sharding import PartitionSpec as P

MESH = pl.DeviceIdType.MESH


def routed(tokens, routes, gates, w_gate, w_up, hidden_grad):
    group_count = lax.axis_size("grp")
    member_count = lax.axis_size("exp")
    experts = group_count * member_count
    tok_rows, part_width = tokens.shape
    per_token = routes.shape[1]
    slots = hidden_grad.shape[1]
    capacity = slots // experts
    flat_routes = routes.reshape(-1)
    onehot = (flat_routes[:, None] == jnp.arange(experts, dtype=jnp.int32)[None, :]).astype(
        jnp.int32
    )
    slot_ranks = jnp.sum((jnp.cumsum(onehot, axis=0) - onehot) * onehot, axis=1)
    blank_row = jnp.zeros((1, part_width), tokens.dtype)
    owner_row = jnp.arange(tok_rows * per_token, dtype=jnp.int32) // per_token
    slot_table = jnp.full((experts * capacity,), tok_rows, jnp.int32)
    slot_table = slot_table.at[flat_routes * capacity + slot_ranks].set(owner_row)
    outgoing = jnp.concatenate([tokens, blank_row], 0)[slot_table].reshape(
        group_count, member_count, capacity, part_width
    )
    across = lax.all_to_all(outgoing, "grp", split_axis=0, concat_axis=0, tiled=True)
    arrived = lax.all_to_all(across, "exp", split_axis=1, concat_axis=1, tiled=True)
    slot_rows = arrived.reshape(slots, part_width)
    weight_gate = w_gate[0]
    weight_up = w_up[0]
    piece = lax.all_gather(slot_rows, "tp", axis=1, tiled=True)
    pre_gate = jnp.dot(piece, weight_gate, preferred_element_type=jnp.float32)
    pre_up = jnp.dot(piece, weight_up, preferred_element_type=jnp.float32)
    sigmoid_gate = jax.nn.sigmoid(pre_gate)
    upstream = hidden_grad[0].astype(jnp.float32)
    grad_gate = (upstream * pre_up * sigmoid_gate * (1.0 + pre_gate * (1.0 - sigmoid_gate))).astype(
        jnp.bfloat16
    )
    grad_up = (upstream * pre_gate * sigmoid_gate).astype(jnp.bfloat16)
    contract = (((1,), (1,)), ((), ()))
    slot_term = lax.dot_general(
        grad_gate, weight_gate, contract, preferred_element_type=jnp.float32
    )
    slot_term = slot_term + lax.dot_general(
        grad_up, weight_up, contract, preferred_element_type=jnp.float32
    )
    summed = lax.psum_scatter(slot_term.astype(jnp.bfloat16), "tp", scatter_dimension=1, tiled=True)
    returned = lax.all_to_all(
        summed.reshape(group_count, member_count, capacity, part_width),
        "exp",
        split_axis=1,
        concat_axis=1,
        tiled=True,
    )
    at_owner = lax.all_to_all(returned, "grp", split_axis=0, concat_axis=0, tiled=True).reshape(
        experts * capacity, part_width
    )
    picked = at_owner[flat_routes * capacity + slot_ranks].reshape(tok_rows, per_token, part_width)
    combined = jnp.sum(gates.astype(jnp.float32)[:, :, None] * picked.astype(jnp.float32), axis=1)
    return combined.astype(jnp.bfloat16)


def dense_kernel(
    tok_hbm, routes_hbm, gt, wg_hbm, wu_hbm, hid_hbm, out_ref,
    rt, hid, w, x, gate_all, pre, grads, p_sib, r_sib, p_own, stage, recv, c_send, c_recv,
    local_sem, send_sem, recv_sem,
):
    n_exp = 4
    rows, width = tok_hbm.shape
    half = width // 2
    group = n_exp * rows
    ht = hid.shape[1]
    gx, ez, tp = lax.axis_index("grp"), lax.axis_index("exp"), lax.axis_index("tp")
    core = lax.rem(tp, 2)
    ty = tp // 2
    ox, oy, oc = 1 - gx, 1 - ty, 1 - core
    zk = [ez, ez + 1 - 2 * lax.rem(ez, 2), lax.rem(ez + 2, n_exp), n_exp - 1 - ez]
    q = 2 * ty + core
    qy = 2 * oy + core
    qc = 2 * ty + oc
    qcy = 2 * oy + oc
    to_x, to_y, to_c = (ox, ez, tp), (gx, ez, qy), (gx, ez, qc)
    to_z = [(gx, z, tp) for z in zk]

    def row(gr, z):
        return pl.multiple_of((gr * n_exp + z) * rows, rows)

    counter = [0]
    sent = []

    def remote(src, dst, device):
        i = counter[0]
        counter[0] += 1
        c = pltpu.make_async_remote_copy(
            src_ref=src, dst_ref=dst, send_sem=send_sem.at[i], recv_sem=recv_sem.at[i],
            device_id=device, device_id_type=MESH,
        )
        c.start()
        sent.append(c)
        return c

    mine = pl.ds(row(gx, ez), rows)
    loc = [
        pltpu.make_async_copy(tok_hbm.at[:, pl.ds(0, half)], x.at[2 * q, mine, :], local_sem.at[0]),
        pltpu.make_async_copy(tok_hbm.at[:, pl.ds(half, half)], x.at[2 * q + 1, mine, :], local_sem.at[1]),
        pltpu.make_async_copy(routes_hbm, rt, local_sem.at[2]),
        pltpu.make_async_copy(wg_hbm, w.at[:, :, pl.ds(0, ht)], local_sem.at[3]),
        pltpu.make_async_copy(wu_hbm, w.at[:, :, pl.ds(ht, ht)], local_sem.at[4]),
        pltpu.make_async_copy(hid_hbm, hid, local_sem.at[5]),
    ]
    for c in loc[:3]:
        c.start()
    barrier = pltpu.get_barrier_semaphore()
    partners = [to_x, to_y, to_c] + to_z[1:]
    for d in partners:
        pl.semaphore_signal(barrier, inc=1, device_id=d, device_id_type=MESH)
    loc[0].wait()
    loc[1].wait()
    pl.semaphore_wait(barrier, len(partners))

    def block(quarter, gr, z):
        return x.at[pl.ds(2 * quarter, 2), pl.ds(row(gr, z), rows), :]

    def piece(quarter, h, gr, z):
        return x.at[2 * quarter + h, pl.ds(row(gr, z), rows), :]

    def same(ref, device):
        return remote(ref, ref, device)

    xc, yc, fa, fb = [None] * 4, [None] * 4, [None] * 4, [None] * 4
    core_copies = [[None] * 4 for _ in range(4)]
    zc = [None] + [same(block(q, gx, ez), to_z[k]) for k in (1, 2, 3)]

    def column(k):
        if k:
            zc[k].wait_recv()
        xc[k] = same(block(q, gx, zk[k]), to_x)
        yc[k] = same(block(q, gx, zk[k]), to_y)
        core_copies[0][k] = same(block(q, gx, zk[k]), to_c)

    def onward(k):
        xc[k].wait_recv()
        fa[k] = same(piece(q, 0, ox, zk[k]), to_y)
        core_copies[1][k] = same(block(q, ox, zk[k]), to_c)
        yc[k].wait_recv()
        fb[k] = same(piece(qy, 1, gx, zk[k]), to_x)
        core_copies[2][k] = same(block(qy, gx, zk[k]), to_c)

    column(0)
    for c in loc[3:]:
        c.start()
    loc[2].wait()
    lanes = lax.broadcasted_iota(jnp.int32, (rows, 128), 1).astype(jnp.float32)
    table = jnp.zeros((rows, 128), jnp.float32)
    chosen = rt[...].astype(jnp.float32)
    values = gt[...].astype(jnp.float32)
    shape = (rows, rows)
    eye = lax.broadcasted_iota(jnp.int32, shape, 0) == lax.broadcasted_iota(jnp.int32, shape, 1)

    def upright(line):
        return jnp.sum(jnp.where(eye, line, 0.0), axis=1, keepdims=True)

    for k in range(chosen.shape[0]):
        pick = lanes == upright(chosen[k : k + 1, :])
        table = table + jnp.where(pick, upright(values[k : k + 1, :]), 0.0)
    gate_all[mine, :] = table.astype(jnp.bfloat16)
    own_gates = gate_all.at[mine, :]
    gz = [same(own_gates, to_z[k]) for k in (1, 2, 3)]
    onward(0)
    column(1)
    column(2)
    onward(1)
    column(3)
    for c in gz:
        c.wait_recv()
    gate_column = gate_all.at[pl.ds(row(gx, 0), group), :]
    gcol = same(gate_column, to_x)
    onward(2)
    onward(3)
    for c in loc[3:]:
        c.wait()

    def first(quarter):
        return jnp.dot(
            x[2 * quarter], w[2 * quarter], preferred_element_type=jnp.float32
        ) + jnp.dot(x[2 * quarter + 1], w[2 * quarter + 1], preferred_element_type=jnp.float32)

    pre[...] = first(q)
    for k in range(4):
        fa[k].wait_recv()
        fb[k].wait_recv()
        core_copies[3][k] = same(block(qy, ox, zk[k]), to_c)
    pre[...] += first(qy)
    for k in range(4):
        core_copies[0][k].wait_recv()
        core_copies[1][k].wait_recv()
    pre[...] += first(qc)
    gcol.wait_recv()
    expert = gx * n_exp + ez
    total_rows = pre.shape[0]
    lane = lax.broadcasted_iota(jnp.int32, (total_rows, 128), 1)
    scale = jnp.sum(
        jnp.where(lane == expert, gate_all[...].astype(jnp.float32), 0.0), axis=1, keepdims=True
    )
    for k in range(4):
        core_copies[2][k].wait_recv()
        core_copies[3][k].wait_recv()
    both = pre[...] + first(qcy)
    pre_gate, pre_up = both[:, :ht], both[:, ht:]
    sg = jax.nn.sigmoid(pre_gate)
    up = hid[...].astype(jnp.float32) * scale * sg
    grads[:, :ht] = (up * pre_up * (1.0 + pre_gate * (1.0 - sg))).astype(jnp.bfloat16)
    grads[:, ht:] = (up * pre_gate).astype(jnp.bfloat16)

    def second(part):
        return lax.dot_general(
            grads[...], w[part], (((1,), (1,)), ((), ())), preferred_element_type=jnp.float32
        )

    sib = []
    for j in range(4):
        p_sib[j] = second(2 * (qcy if j < 2 else qc) + j % 2).astype(jnp.bfloat16)
        sib.append(remote(p_sib.at[j], r_sib.at[j], to_c))
    for j in (0, 1):
        p_own[j] = second(2 * qy + j)
    da, db, sx, sy = {}, {}, {}, {}

    def own(j, gr, k):
        at = pl.ds(row(gr, zk[k]), rows)
        return p_own[j, at, :] + r_sib[j, at, :].astype(jnp.float32)

    def got(slot, k):
        return recv[slot, k].astype(jnp.float32)

    def send(slot, value, k, device):
        stage[slot, k] = value.astype(jnp.bfloat16)
        return remote(stage.at[slot, k], recv.at[slot, k], device)

    def diagonal(k):
        da[k] = send(0, own(0, ox, k), k, to_y)
        db[k] = send(1, own(1, ox, k), k, to_x)

    def plain(k):
        sy[0, k] = send(2, own(0, gx, k), k, to_y)
        sx[1, k] = send(3, own(3, ox, k), k, to_x)

    def joined(k):
        da[k].wait_recv()
        sx[0, k] = send(4, own(2, ox, k) + got(0, k), k, to_x)
        db[k].wait_recv()
        sy[1, k] = send(5, own(1, gx, k) + got(1, k), k, to_y)

    back, mine_sum = {}, [None, None]

    def finish(k):
        for c in (sy[0, k], sx[1, k], sx[0, k], sy[1, k]):
            c.wait_recv()
        for h, slots in ((0, (4, 2)), (1, (3, 5))):
            v = own(2 + h, gx, k) + got(slots[0], k) + got(slots[1], k)
            if k:
                c_send[k - 1, h] = v.astype(jnp.bfloat16)
            else:
                mine_sum[h] = v
        if k:
            back[k] = remote(c_send.at[k - 1], c_recv.at[k - 1], to_z[k])

    sib[0].wait_recv()
    sib[1].wait_recv()
    diagonal(2)
    diagonal(3)
    diagonal(1)
    diagonal(0)
    for j in (2, 3):
        p_own[j] = second(2 * q + j % 2)
    sib[2].wait_recv()
    sib[3].wait_recv()
    plain(2)
    plain(3)
    joined(2)
    joined(3)
    plain(1)
    plain(0)
    joined(1)
    joined(0)
    for k in (2, 3, 1, 0):
        finish(k)
    for k in (1, 2, 3):
        back[k].wait_recv()
    for h in range(2):
        v = mine_sum[h]
        for k in range(3):
            v = v + c_recv[k, h].astype(jnp.float32)
        out_ref[:, h * half : (h + 1) * half] = v.astype(jnp.bfloat16)
    for c in sent:
        c.wait_send()


def dense(tokens, routes, gates, w_gate, w_up, hidden_grad):
    rows, width = tokens.shape
    half = width // 2
    _, depth, ht = w_gate.shape
    slots = hidden_grad.shape[1]
    parts = depth // half
    bf16, f32 = jnp.bfloat16, jnp.float32
    any_space = pl.BlockSpec(memory_space=pl.ANY)
    n_copies = 3 + 8 + 8 + 16 + 4 + 4 + 24 + 3
    return pl.pallas_call(
        dense_kernel,
        out_shape=jax.ShapeDtypeStruct((rows, width), bf16),
        in_specs=[any_space] * 2 + [pl.BlockSpec(memory_space=pltpu.VMEM)] + [any_space] * 3,
        out_specs=pl.BlockSpec(memory_space=pltpu.VMEM),
        scratch_shapes=[
            pltpu.VMEM(routes.shape[::-1], jnp.int32),
            pltpu.VMEM((slots, ht), bf16),
            pltpu.VMEM((parts, half, 2 * ht), bf16),
            pltpu.VMEM((parts, slots, half), bf16),
            pltpu.VMEM((slots, 128), bf16),
            pltpu.VMEM((slots, 2 * ht), f32),
            pltpu.VMEM((slots, 2 * ht), bf16),
            pltpu.VMEM((4, slots, half), bf16),
            pltpu.VMEM((4, slots, half), bf16),
            pltpu.VMEM((4, slots, half), f32),
            pltpu.VMEM((6, 4, rows, half), bf16),
            pltpu.VMEM((6, 4, rows, half), bf16),
            pltpu.VMEM((3, 2, rows, half), bf16),
            pltpu.VMEM((3, 2, rows, half), bf16),
            pltpu.SemaphoreType.DMA((6,)),
            pltpu.SemaphoreType.DMA((n_copies,)),
            pltpu.SemaphoreType.DMA((n_copies,)),
        ],
        compiler_params=pltpu.CompilerParams(
            collective_id=0, has_side_effects=True, vmem_limit_bytes=56 << 20
        ),
        cost_estimate=pl.CostEstimate(
            flops=8 * slots * depth * ht, bytes_accessed=4 * depth * ht, transcendentals=slots * ht
        ),
    )(
        tokens,
        routes.T,
        gates.T,
        w_gate.reshape(parts, half, ht),
        w_up.reshape(parts, half, ht),
        hidden_grad.reshape(slots, ht),
    )


def solution(mesh):
    placed = (
        P(("grp", "exp"), "tp"),
        P(("grp", "exp"), None),
        P(("grp", "exp"), None),
        P(("grp", "exp"), None, "tp"),
        P(("grp", "exp"), None, "tp"),
        P(("grp", "exp"), None, "tp"),
    )
    sizes = (mesh.shape["grp"], mesh.shape["exp"], mesh.shape["tp"])
    experts = sizes[0] * sizes[1]

    def local(tokens, routes, *rest):
        if sizes == (2, 4, 4) and routes.shape[1] == experts:
            return dense(tokens, routes, *rest)
        return routed(tokens, routes, *rest)

    return jax.shard_map(
        local, mesh=mesh, in_specs=placed, out_specs=P(("grp", "exp"), "tp"), check_vma=False
    )
```
